512 devices in a mesh: dp: 512 (over y, x, z, core).
Axes of the slice: x: 4, y: 4, z: 16, core: 2. Of those that a mesh axis runs over, the one named last changes fastest.
Arguments:
- picture_embedding: float32 [196608, 768], P('dp'), may hold values from -0.3 to 0.3
- caption_embedding: float32 [196608, 768], P('dp'), may hold values from -0.3 to 0.3
- match_class_tags: int32 [196608], P('dp'), may hold values from 0 to 49151
- natural_log_heat: float32 [1], replicated, may hold values from 1.5 to 2.5
- offset_term: float32 [1], replicated, may hold values from -3 to -1
Outputs:
- picture_sensitivity: float32 [196608, 768], P('dp')
- caption_sensitivity: float32 [196608, 768], P('dp')
The draws below stay inside these ranges and needn't reach their ends.
All inputs are finite; a program needn't handle non-finite values.
Results may differ from the reference program's by a relative error of at most 0.0003.
Values sent between devices are 32-bit elements; how exact they have to be, the bound alone decides.
No kernel may reach another device: no remote copies, remote signals or barrier semaphores. Data moves between devices by JAX's collectives and lax.ppermute only.
A program may use at most 64 MiB of HBM per device.

```python
import jax
import jax.numpy as jnp
from jax import lax

D = 768
ROWS = 384
ROUND_ONE = 1
ROUND_TWO = 256
TOTAL = 196608
N_DP = 512


def set_ends(result, rng, least, high):
    shape = result.shape
    index_at = [jax.random.randint(jax.random.fold_in(rng, axis), (), 0, shape[axis]) for axis in range(len(shape))]
    result = result.at[tuple(index_at)].set(least)
    longest = shape.index(max(shape))
    index_at[longest] = (index_at[longest] + 1) % shape[longest]
    return result.at[tuple(index_at)].set(high)


def block_scale(stream_key, dims, shards, least, largest):
    def one(axis_at, parts):
        steps = jax.random.uniform(jax.random.fold_in(jax.random.fold_in(stream_key, 6), axis_at), (parts,), jnp.float32, least / len(shards), largest / len(shards))
        return jnp.repeat(jnp.exp(steps), dims[axis_at] // parts).reshape((-1,) + (1,) * (len(dims) - axis_at - 1))

    gain = one(*shards[0])
    for cut in shards[1:]:
        gain = gain * one(*cut)
    return gain


def normal_values(key, dims, scale, most, pieces=(), held_as=jnp.bfloat16):
    entries = scale * jax.random.normal(key, dims, jnp.float32)
    if pieces:
        entries = entries * block_scale(key, dims, pieces, -0.22, 0.18)
    return jnp.clip(entries, -most, most).astype(held_as)


def setup_inputs(seed: int = 0) -> dict:
    keys = jax.random.split(jax.random.key(seed), 6)
    return {
        "picture_embedding": normal_values(keys[0], (TOTAL, D), 0.05, 0.3, ((0, 512),), jnp.float32),
        "caption_embedding": normal_values(keys[1], (TOTAL, D), 0.05, 0.3, ((0, 512),), jnp.float32),
        "match_class_tags": set_ends(jax.random.randint(keys[2], (TOTAL,), 0, ROWS * N_DP // 4), jax.random.fold_in(keys[2], 1), 0, (ROWS * N_DP // 4) - 1).astype(jnp.int32),
        "natural_log_heat": jnp.clip(jax.random.uniform(keys[3], (1,), jnp.float32, 1.5, 2.5), 1.5, 2.5),
        "offset_term": jnp.clip(jax.random.uniform(keys[4], (1,), jnp.float32, -3.0, -1.0), -3.0, -1.0),
    }


def normalize(rows):
    return rows * lax.rsqrt(lax.optimization_barrier(jnp.sum(rows * rows, axis=-1, keepdims=True)) + 1e-06)

def tile_slopes(former_peer, latter_peer, former_class_tags, latter_class_tags, sharpness_factor, tile_shift_amount):
    similarity_matrix = sharpness_factor * jnp.dot(former_peer, latter_peer.T, precision=lax.Precision.HIGHEST, preferred_element_type=jnp.float32) + tile_shift_amount
    labels = jnp.where(former_class_tags[:, None] == latter_class_tags[None, :], 1.0, -1.0).astype(jnp.float32)
    return -labels * jax.nn.sigmoid(-labels * similarity_matrix)

def reference(picture_embedding, caption_embedding, match_class_tags, natural_log_heat, offset_term):
    sharpness_factor = jnp.exp(natural_log_heat[0])
    tile_shift_amount = offset_term[0]
    unit_image_rows, incoming_picture = jax.vjp(normalize, picture_embedding)
    unit_text_rows, incoming_caption = jax.vjp(normalize, caption_embedding)
    group = N_DP
    picture_tiles = unit_image_rows.reshape(group, ROWS, D)
    caption_tiles = unit_text_rows.reshape(group, ROWS, D)
    class_tag_tiles = match_class_tags.reshape(group, ROWS)
    offsets = (0, ROUND_ONE, ROUND_TWO)

    def per_device(device):
        resident_picture = picture_tiles[device]
        resident_caption = caption_tiles[device]
        resident_class_tags = class_tag_tiles[device]
        picture_pull = jnp.zeros((ROWS, D), jnp.float32)
        caption_pull = jnp.zeros((ROWS, D), jnp.float32)
        for step in offsets:
            source_peer_number = ((device - step) % group).astype(jnp.int32)
            similarity_slopes = tile_slopes(resident_picture, caption_tiles[source_peer_number], resident_class_tags, class_tag_tiles[source_peer_number], sharpness_factor, tile_shift_amount)
            picture_pull = picture_pull + jnp.dot(similarity_slopes, caption_tiles[source_peer_number], precision=lax.Precision.HIGHEST, preferred_element_type=jnp.float32)
            target_peer_number = ((device + step) % group).astype(jnp.int32)
            similarity_slopes = tile_slopes(picture_tiles[target_peer_number], resident_caption, class_tag_tiles[target_peer_number], resident_class_tags, sharpness_factor, tile_shift_amount)
            caption_pull = caption_pull + jnp.dot(similarity_slopes.T, picture_tiles[target_peer_number], precision=lax.Precision.HIGHEST, preferred_element_type=jnp.float32)
        return (sharpness_factor * picture_pull, sharpness_factor * caption_pull)
    picture_pull, caption_pull = lax.map(per_device, jnp.arange(group, dtype=jnp.int32))
    picture_sensitivity = incoming_picture(picture_pull.reshape(group * ROWS, D))[0]
    caption_sensitivity = incoming_caption(caption_pull.reshape(group * ROWS, D))[0]
    return (picture_sensitivity, caption_sensitivity)
```

```python
import functools

import jax
import jax.numpy as jnp
from jax import lax
from jax.experimental import pallas as pl
from jax.experimental.pallas import tpu as pltpu
from jax.sharding import PartitionSpec as P

NT = (((1,), (1,)), ((), ()))
NN = (((1,), (0,)), ((), ()))
PLANE = 128
DEEP = 16
RELAYS = ((0, 15), (3, 0))
PARTS = len(RELAYS) + 1
VMEM = pl.BlockSpec(memory_space=pltpu.VMEM)
SMEM = pl.BlockSpec(memory_space=pltpu.SMEM)


def shift(block, distance, skip=False):
    count = lax.axis_size("dp")
    route = [(i, (i + distance) % count) for i in range(count)]
    if skip:
        route = [(i, j) for i, j in route if i // PLANE == j // PLANE]
    return lax.ppermute(block, "dp", route)


def relay(column, core):
    return (column[0] * DEEP + column[1]) * 2 + core


def outward(block, column):
    count = lax.axis_size("dp")
    up = 0 if column is None else relay(column, 0)
    down = PLANE - 1 if column is None else relay(column, 1)
    route = []
    for plane in range(0, count, PLANE):
        route.append((plane + PLANE - 1, (plane + PLANE) % count + up))
        route.append((plane, (plane - PLANE) % count + down))
    return lax.ppermute(block, "dp", route)


def homeward(block, column):
    count = lax.axis_size("dp")
    route = []
    for plane in range(0, count, PLANE):
        route.append((plane + relay(column, 0), plane))
        route.append((plane + relay(column, 1), plane + PLANE - 1))
    return lax.ppermute(block, "dp", route)


def inverse_norm(rows):
    return lax.rsqrt(jnp.sum(rows * rows, axis=-1, keepdims=True) + 1e-06)


def halves(value):
    high = value.astype(jnp.bfloat16)
    low = (value - high.astype(jnp.float32)).astype(jnp.bfloat16)
    return high, low


def dot3(left, right, dims):
    dot = functools.partial(lax.dot_general, dimension_numbers=dims, preferred_element_type=jnp.float32)
    return dot(left[0], right[0]) + (dot(left[0], right[1]) + dot(left[1], right[0]))


def column_of(row):
    return jnp.transpose(jnp.broadcast_to(row, (8, row.shape[1])))[:, :1]


def slopes(own, other, own_tags, other_tags, heat, bias):
    logit = heat * dot3(own, other, NT) + bias
    same = own_tags == other_tags
    slope = 1.0 / (1.0 + jnp.exp(jnp.where(same, logit, -logit)))
    return jnp.where(same, -slope, slope)


def pull(own, other, *tags_and_scalars):
    return dot3(halves(slopes(own, other, *tags_and_scalars)), other, NN)


def scalars(heat_ref, bias_ref):
    return jnp.exp(jnp.full((1, 1), heat_ref[0], jnp.float32)), bias_ref[0]


def through_norm(total, unit, scale, heat):
    total = heat * total
    return scale * (total - unit * jnp.sum(unit * total, axis=-1, keepdims=True))


def put_tags(ref, tags):
    count = ref.shape[0] - 8
    ref[count:, :] = jnp.zeros((8, ref.shape[1]), jnp.float32)
    ref[count : count + 1, : tags.shape[1]] = tags


def unit_kernel(
    caption_ref, picture_ref, tags_ref,
    caption_out, picture_out, caption_scale, picture_scale, *refs,
):
    parts, (raw, sem) = refs[:PARTS], refs[PARTS:]
    rows = tags_ref.shape[1]
    first = pltpu.make_async_copy(caption_ref, raw.at[0], sem.at[0])
    second = pltpu.make_async_copy(picture_ref, raw.at[1], sem.at[1])
    first.start()
    second.start()
    tags = tags_ref[...].astype(jnp.float32)
    place = lax.rem(lax.axis_index("dp"), PLANE)
    for k, (copy, out, scale_out) in enumerate(
        ((first, caption_out, caption_scale), (second, picture_out, picture_scale))
    ):
        copy.wait()
        value = raw[k]
        scale = inverse_norm(value)
        out[:rows, :] = value * scale
        put_tags(out, tags)
        scale_out[...] = jnp.broadcast_to(scale, scale_out.shape)

    def cut(source):
        step = rows // PARTS
        for k, part in enumerate(parts):
            part[:step, :] = source[k * step : (k + 1) * step, :]
        put_tags(parts[0], tags)

    @pl.when(place == PLANE - 1)
    def _():
        cut(caption_out)

    @pl.when(place == 0)
    def _():
        cut(picture_out)


def own_kernel(
    heat_ref, bias_ref, caption_ref, picture_ref,
    picture_high_ref, picture_low_ref, caption_high_ref, caption_low_ref, p_ref, c_ref,
):
    heat, bias = scalars(heat_ref, bias_ref)
    rows = p_ref.shape[0]
    tags = caption_ref[rows : rows + 1, :rows]
    picture, caption = halves(picture_ref[:rows, :]), halves(caption_ref[:rows, :])
    picture_high_ref[...], picture_low_ref[...] = picture
    caption_high_ref[...], caption_low_ref[...] = caption
    slope = slopes(picture, caption, column_of(tags), tags, heat, bias)
    p_ref[...] = dot3(halves(slope), caption, NN)
    c_ref[...] = dot3(halves(jnp.transpose(slope)), picture, NN)


def far_caption_kernel(heat_ref, bias_ref, own_ref, high_ref, low_ref, far_ref, in_ref, out_ref):
    heat, bias = scalars(heat_ref, bias_ref)
    rows = out_ref.shape[0]
    own_tags = column_of(own_ref[rows : rows + 1, :rows])
    tags = far_ref[rows : rows + 1, :rows]
    other = halves(far_ref[:rows, :])
    out_ref[...] = in_ref[...] + pull((high_ref[...], low_ref[...]), other, own_tags, tags, heat, bias)


def far_picture_kernel(
    heat_ref, bias_ref, own_ref, scale_ref, high_ref, low_ref, far_ref, in_ref, out_ref
):
    heat, bias = scalars(heat_ref, bias_ref)
    rows = out_ref.shape[0]
    own_tags = column_of(own_ref[rows : rows + 1, :rows])
    tags = far_ref[rows : rows + 1, :rows]
    other = halves(far_ref[:rows, :])
    total = in_ref[...] + pull((high_ref[...], low_ref[...]), other, own_tags, tags, heat, bias)
    out_ref[...] = through_norm(total, own_ref[:rows, :], scale_ref[:, :1], heat)


def near_kernel(
    heat_ref, bias_ref, picture_ref, scale_ref,
    picture_high_ref, picture_low_ref, caption_high_ref, caption_low_ref,
    near_caption_ref, near_picture_ref, p_in_ref, c_in_ref, *refs,
):
    parts, (p_ref, c_ref, block) = refs[:PARTS], refs[PARTS:]
    heat, bias = scalars(heat_ref, bias_ref)
    rows = p_ref.shape[0]
    own_tags = column_of(picture_ref[rows : rows + 1, :rows])
    place = lax.rem(lax.axis_index("dp"), PLANE)

    def whole(near_ref, relayed):
        @pl.when(relayed)
        def _():
            step = rows // PARTS
            for k, part in enumerate(parts):
                block[k * step : (k + 1) * step, :] = part[:step, :]
            block[rows:, :] = parts[0][step:, :]

        @pl.when(jnp.logical_not(relayed))
        def _():
            block[...] = near_ref[...]

        return halves(block[:rows, :]), block[rows : rows + 1, :rows]

    other, tags = whole(near_caption_ref, place == 0)
    own = picture_high_ref[...], picture_low_ref[...]
    total = p_in_ref[...] + pull(own, other, own_tags, tags, heat, bias)
    p_ref[...] = through_norm(total, picture_ref[:rows, :], scale_ref[:, :1], heat)
    other, tags = whole(near_picture_ref, place == PLANE - 1)
    own = caption_high_ref[...], caption_low_ref[...]
    c_ref[...] = c_in_ref[...] + pull(own, other, own_tags, tags, heat, bias)


def call(kernel, out_shape, *operands, in_hbm=0, scratch=()):
    specs = [pl.BlockSpec(memory_space=pl.ANY)] * in_hbm
    specs += [SMEM if x.size == 1 else VMEM for x in operands[in_hbm:]]
    return pl.pallas_call(
        kernel,
        out_shape=out_shape,
        in_specs=specs,
        out_specs=[VMEM] * len(out_shape),
        scratch_shapes=scratch,
        compiler_params=pltpu.CompilerParams(vmem_limit_bytes=24 * 1024 * 1024),
        cost_estimate=pl.CostEstimate(flops=1024, bytes_accessed=1024, transcendentals=0),
    )(*operands)


def local(picture, caption, tags, heat, bias):
    half = lax.axis_size("dp") // 2
    rows, width = picture.shape
    step = rows // PARTS

    def f32(n, m=width):
        return jax.ShapeDtypeStruct((n, m), jnp.float32)

    def b16(n):
        return jax.ShapeDtypeStruct((n, width), jnp.bfloat16)

    caption, picture, caption_scale, picture_scale, *parts = call(
        unit_kernel,
        [f32(rows + 8)] * 2 + [f32(rows, 128)] * 2 + [f32(step + 8)] + [f32(step)] * (PARTS - 1),
        caption, picture, tags[None, :],
        in_hbm=2,
        scratch=[pltpu.VMEM((2, rows, width), jnp.float32), pltpu.SemaphoreType.DMA((2,))],
    )
    far_caption = shift(caption, half)
    far_picture = shift(picture, half)
    parts = [outward(part, to) for part, to in zip(parts, (None, *RELAYS), strict=True)]
    parts[1:] = [homeward(part, by) for part, by in zip(parts[1:], RELAYS, strict=True)]
    near_caption = shift(caption, 1, skip=True)
    near_picture = shift(picture, -1, skip=True)
    *units, p, c = call(
        own_kernel, [b16(rows)] * 4 + [f32(rows)] * 2, heat, bias, caption, picture
    )
    (p,) = call(
        far_caption_kernel, [f32(rows)], heat, bias, picture, *units[:2], far_caption, p
    )
    p, c = call(
        near_kernel, [f32(rows)] * 2,
        heat, bias, picture, picture_scale, *units, near_caption, near_picture, p, c, *parts,
        scratch=[pltpu.VMEM((rows + 8, width), jnp.float32)],
    )
    (c,) = call(
        far_picture_kernel, [f32(rows)],
        heat, bias, caption, caption_scale, *units[2:], far_picture, c,
    )
    return p, c


def solution(mesh):
    return jax.shard_map(
        local,
        mesh=mesh,
        in_specs=(P("dp", None), P("dp", None), P("dp"), P(), P()),
        out_specs=(P("dp", None), P("dp", None)),
        check_vma=False,
    )
```

```python
import jax
import jax.numpy as jnp
from jax import lax
from jax.experimental import pallas as pl
from jax.experimental.pallas import tpu as pltpu
from jax.sharding import PartitionSpec as P

NT = (((1,), (1,)), ((), ()))
NN = (((1,), (0,)), ((), ()))
PLANE = 128
DEEP = 16
UP_BY = ((0, 15), (3, 0), (2, 15), (3, 14))
DOWN_BY = ((0, 15), (3, 0), (1, 0), (0, 1))
PARTS = len(UP_BY)
FAR_COST = 1 << 37
VMEM = pl.BlockSpec(memory_space=pltpu.VMEM)
SMEM = pl.BlockSpec(memory_space=pltpu.SMEM)


def swap(block, to):
    count = lax.axis_size("dp")
    route = [(i, to(i) % count) for i in range(count)]
    return lax.ppermute(block, "dp", [pair for pair in route if pair[0] != pair[1]])


def over_core(i):
    return i ^ 1


def over_chip(i):
    j = i + 1 if i % 2 else i - 1
    return j if i // PLANE == j // PLANE else i


def relays(k):
    up, down = UP_BY[k], DOWN_BY[k]
    return (up[0] * DEEP + up[1]) * 2, (down[0] * DEEP + down[1]) * 2 + 1


def outward(block, k):
    count = lax.axis_size("dp")
    up, down = relays(k)
    route = []
    for plane in range(0, count, PLANE):
        route.append((plane + PLANE - 1, (plane + PLANE) % count + up))
        route.append((plane, (plane - PLANE) % count + down))
    return lax.ppermute(block, "dp", route)


def homeward(block, k):
    count = lax.axis_size("dp")
    up, down = relays(k)
    route = []
    for plane in range(0, count, PLANE):
        route.append((plane + up, plane))
        route.append((plane + down, plane + PLANE - 1))
    return lax.ppermute(block, "dp", route)


def inverse_norm(rows):
    return lax.rsqrt(jnp.sum(rows * rows, axis=-1, keepdims=True) + 1e-06)


def halves(value):
    high = value.astype(jnp.bfloat16)
    low = (value - high.astype(jnp.float32)).astype(jnp.bfloat16)
    return high, low


def dot(left, right, dims):
    return lax.dot_general(left, right, dims, preferred_element_type=jnp.float32)


def dot_nt(left, right):
    count = right[0].shape[0]
    both = dot(left[0], jnp.concatenate(right, axis=0), NT)
    return both[:, :count] + (both[:, count:] + dot(left[1], right[0], NT))


def dot_nn(left, right):
    high, low = right
    left = jnp.concatenate([left[0], left[0], left[1]], axis=1)
    return dot(left, jnp.concatenate([high, low, high], axis=0), NN)


def column_of(row):
    return jnp.transpose(jnp.broadcast_to(row, (8, row.shape[1])))[:, :1]


def slopes(own, other, own_tags, other_tags, heat, bias):
    logit = heat * dot_nt(own, other) + bias
    return 1.0 / (1.0 + jnp.exp(-logit)) - jnp.where(own_tags == other_tags, 1.0, 0.0)


def pull(own, other, *tags_and_scalars):
    return dot_nn(halves(slopes(own, other, *tags_and_scalars)), other)


def scalars(heat_ref, bias_ref):
    return jnp.exp(jnp.full((1, 1), heat_ref[0], jnp.float32)), bias_ref[0]


def through_norm(total, unit, scale, heat):
    total = heat * total
    return scale * (total - unit * jnp.sum(unit * total, axis=-1, keepdims=True))


def put_tags(ref, tags):
    count = ref.shape[0] - 8
    ref[count:, :] = jnp.zeros((8, ref.shape[1]), jnp.float32)
    ref[count : count + 1, : tags.shape[1]] = tags


def is_even():
    return lax.rem(lax.axis_index("dp"), 2) == 0


def stage_kernel(caption_ref, tags_ref, out_ref):
    out_ref[: caption_ref.shape[0], :] = caption_ref[...]
    put_tags(out_ref, tags_ref[...].astype(jnp.float32))


def unit_kernel(
    staged_ref, picture_ref,
    caption_out, picture_out, core_out, chip_out, own_tags_out, caption_scale, picture_scale, *parts,
):
    rows = picture_ref.shape[0]
    even = is_even()
    tags = staged_ref[rows : rows + 1, :rows]
    own_tags_out[...] = jnp.broadcast_to(column_of(tags), own_tags_out.shape)
    units = []
    for source, out, scale_out in (
        (staged_ref, caption_out, caption_scale),
        (picture_ref, picture_out, picture_scale),
    ):
        value = source[:rows, :]
        scale = inverse_norm(value)
        units.append(value * scale)
        out[...] = units[-1]
        scale_out[...] = jnp.broadcast_to(scale, scale_out.shape)
    caption, picture = units
    core_out[:rows, :] = jnp.where(even, caption, picture)
    put_tags(core_out, tags)
    chip = jnp.where(even, picture, caption)
    chip_out[:rows, :] = chip
    put_tags(chip_out, tags)
    step = rows // PARTS
    for k, part in enumerate(parts):
        part[:step, :] = chip[k * step : (k + 1) * step, :]
    put_tags(parts[0], tags)


def place_in_plane():
    return lax.rem(lax.axis_index("dp"), PLANE)


def own_kernel(
    heat_ref, bias_ref, own_tags_ref, staged_ref, caption_ref, picture_ref,
    caption_high_ref, caption_low_ref, picture_high_ref, picture_low_ref, c_ref, p_ref,
):
    heat, bias = scalars(heat_ref, bias_ref)
    rows = c_ref.shape[0]
    tags = staged_ref[rows : rows + 1, :rows]
    caption, picture = halves(caption_ref[...]), halves(picture_ref[...])
    caption_high_ref[...], caption_low_ref[...] = caption
    picture_high_ref[...], picture_low_ref[...] = picture
    slope = slopes(caption, picture, own_tags_ref[:, :1], tags, heat, bias)
    c_ref[...] = dot_nn(halves(slope), picture)
    p_ref[...] = dot_nn(halves(jnp.transpose(slope)), caption)


def far_kernel(heat_ref, bias_ref, own_tags_ref, high_ref, low_ref, far_ref, in_ref, out_ref):
    heat, bias = scalars(heat_ref, bias_ref)
    rows = out_ref.shape[0]
    other = far_ref[:rows, :]
    own, other = (high_ref[...], low_ref[...]), halves(other * inverse_norm(other))
    tags = far_ref[rows : rows + 1, :rows]
    out_ref[...] = in_ref[...] + pull(own, other, own_tags_ref[:, :1], tags, heat, bias)


def near_pull(heat, bias, own_tags_ref, caption, picture, of_caption, other_ref):
    rows = other_ref.shape[0] - 8
    own = [jnp.where(of_caption, c[...], p[...]) for c, p in zip(caption, picture, strict=True)]
    tags = other_ref[rows : rows + 1, :rows]
    return pull(own, halves(other_ref[:rows, :]), own_tags_ref[:, :1], tags, heat, bias)


def core_kernel(
    heat_ref, bias_ref, own_tags_ref,
    caption_high_ref, caption_low_ref, picture_high_ref, picture_low_ref,
    other_ref, c_in_ref, p_in_ref, c_ref, p_ref,
):
    heat, bias = scalars(heat_ref, bias_ref)
    even = is_even()
    caption, picture = (caption_high_ref, caption_low_ref), (picture_high_ref, picture_low_ref)
    more = near_pull(heat, bias, own_tags_ref, caption, picture, even, other_ref)
    c_ref[...] = c_in_ref[...] + jnp.where(even, more, 0.0)
    p_ref[...] = p_in_ref[...] + jnp.where(even, 0.0, more)


def chip_kernel(
    heat_ref, bias_ref, own_tags_ref, picture_ref, scale_ref,
    caption_high_ref, caption_low_ref, picture_high_ref, picture_low_ref,
    other_ref, c_in_ref, p_in_ref, *refs,
):
    parts, (c_ref, p_ref, block) = refs[:PARTS], refs[PARTS:]
    heat, bias = scalars(heat_ref, bias_ref)
    rows = c_ref.shape[0]
    step = rows // PARTS
    even = is_even()
    place = place_in_plane()
    in_parts = jnp.logical_or(place == 0, place == PLANE - 1)

    @pl.when(in_parts)
    def _():
        for k, part in enumerate(parts):
            block[k * step : (k + 1) * step, :] = part[:step, :]
        block[rows:, :] = parts[0][step:, :]

    @pl.when(jnp.logical_not(in_parts))
    def _():
        block[...] = other_ref[...]

    caption, picture = (caption_high_ref, caption_low_ref), (picture_high_ref, picture_low_ref)
    more = near_pull(heat, bias, own_tags_ref, caption, picture, jnp.logical_not(even), block)
    c_ref[...] = c_in_ref[...] + jnp.where(even, 0.0, more)
    total = p_in_ref[...] + jnp.where(even, more, 0.0)
    p_ref[...] = through_norm(total, picture_ref[...], scale_ref[:, :1], heat)


def last_kernel(
    heat_ref, bias_ref, own_tags_ref, unit_ref, scale_ref, high_ref, low_ref, far_ref, tags_ref,
    in_ref, out_ref,
):
    heat, bias = scalars(heat_ref, bias_ref)
    rows = out_ref.shape[0]
    own, other = (high_ref[...], low_ref[...]), halves(far_ref[...])
    tags = tags_ref[rows : rows + 1, :rows]
    total = in_ref[...] + pull(own, other, own_tags_ref[:, :1], tags, heat, bias)
    out_ref[...] = through_norm(total, unit_ref[...], scale_ref[:, :1], heat)


def call(kernel, out_shape, *operands, cost=1024, scratch=()):
    return pl.pallas_call(
        kernel,
        out_shape=out_shape,
        in_specs=[SMEM if x.size == 1 else VMEM for x in operands],
        out_specs=[VMEM] * len(out_shape),
        scratch_shapes=scratch,
        compiler_params=pltpu.CompilerParams(vmem_limit_bytes=24 * 1024 * 1024),
        cost_estimate=pl.CostEstimate(flops=cost, bytes_accessed=1024, transcendentals=0),
    )(*operands)


def local(picture, caption, tags, heat, bias):
    count = lax.axis_size("dp")
    rows, width = picture.shape
    step = rows // PARTS

    def f32(n, m=width):
        return jax.ShapeDtypeStruct((n, m), jnp.float32)

    def b16(n):
        return jax.ShapeDtypeStruct((n, width), jnp.bfloat16)

    def over_half(i):
        return i + count // 2

    (staged,) = call(stage_kernel, [f32(rows + 8)], caption, tags[None, :])
    far_caption = swap(staged, over_half)
    caption, picture, core, chip, own_tags, caption_scale, picture_scale, *parts = call(
        unit_kernel,
        [f32(rows)] * 2 + [f32(rows + 8)] * 2 + [f32(rows, 128)] * 3
        + [f32(step + 8)] + [f32(step)] * (PARTS - 1),
        staged, picture,
    )
    parts = [outward(part, k) for k, part in enumerate(parts)]
    parts = [homeward(part, k) for k, part in enumerate(parts)]
    core = swap(core, over_core)
    chip = swap(chip, over_chip)
    far_picture = swap(picture, over_half)
    scalar = heat, bias, own_tags
    *units, c, p = call(
        own_kernel, [b16(rows)] * 4 + [f32(rows)] * 2, *scalar, staged, caption, picture
    )
    (p,) = call(far_kernel, [f32(rows)], *scalar, *units[2:], far_caption, p, cost=FAR_COST)
    c, p = call(core_kernel, [f32(rows)] * 2, *scalar, *units, core, c, p)
    c, p = call(
        chip_kernel, [f32(rows)] * 2,
        *scalar, picture, picture_scale, *units, chip, c, p, *parts,
        scratch=[pltpu.VMEM((rows + 8, width), jnp.float32)],
    )
    (c,) = call(
        last_kernel, [f32(rows)],
        *scalar, caption, caption_scale, *units[:2], far_picture, far_caption, c,
    )
    return p, c


def solution(mesh):
    return jax.shard_map(
        local,
        mesh=mesh,
        in_specs=(P("dp", None), P("dp", None), P("dp"), P(), P()),
        out_specs=(P("dp", None), P("dp", None)),
        check_vma=False,
    )
```

```python
import jax
import jax.numpy as jnp
from jax import lax
from jax.experimental import pallas as pl
from jax.experimental.pallas import tpu as pltpu
from jax.sharding import PartitionSpec as P

NT = (((1,), (1,)), ((), ()))
NN = (((1,), (0,)), ((), ()))
PLANE = 128
DEEP = 16
UP_BY = ((0, 15), (3, 0), (2, 15), (3, 14))
DOWN_BY = ((0, 15), (3, 0), (1, 0), (0, 1))
PARTS = len(UP_BY)
BLOCKS = 3
FAR_COST = 1 << 37
VMEM = pl.BlockSpec(memory_space=pltpu.VMEM)
SMEM = pl.BlockSpec(memory_space=pltpu.SMEM)


def swap(block, to):
    count = lax.axis_size("dp")
    route = [(i, to(i) % count) for i in range(count)]
    return lax.ppermute(block, "dp", [pair for pair in route if pair[0] != pair[1]])


def over_core(i):
    return i ^ 1


def over_chip(i):
    j = i + 1 if i % 2 else i - 1
    return j if i // PLANE == j // PLANE else i


def relays(k):
    up, down = UP_BY[k], DOWN_BY[k]
    return (up[0] * DEEP + up[1]) * 2, (down[0] * DEEP + down[1]) * 2 + 1


def outward(block, k):
    count = lax.axis_size("dp")
    up, down = relays(k)
    route = []
    for plane in range(0, count, PLANE):
        route.append((plane + PLANE - 1, (plane + PLANE) % count + up))
        route.append((plane, (plane - PLANE) % count + down))
    return lax.ppermute(block, "dp", route)


def homeward(block, k):
    count = lax.axis_size("dp")
    up, down = relays(k)
    route = []
    for plane in range(0, count, PLANE):
        route.append((plane + up, plane))
        route.append((plane + down, plane + PLANE - 1))
    return lax.ppermute(block, "dp", route)


def inverse_norm(rows):
    return lax.rsqrt(jnp.sum(rows * rows, axis=-1, keepdims=True) + 1e-06)


def halves(value):
    high = value.astype(jnp.bfloat16)
    low = (value - high.astype(jnp.float32)).astype(jnp.bfloat16)
    return high, low


def dot(left, right, dims):
    return lax.dot_general(left, right, dims, preferred_element_type=jnp.float32)


def dot_nt(left, right):
    count = right[0].shape[0]
    both = dot(left[0], jnp.concatenate(right, axis=0), NT)
    return both[:, :count] + (both[:, count:] + dot(left[1], right[0], NT))


def dot_nn(left, right):
    high, low = right
    left = jnp.concatenate([left[0], left[0], left[1]], axis=1)
    return dot(left, jnp.concatenate([high, low, high], axis=0), NN)


def column_of(row):
    return jnp.transpose(jnp.broadcast_to(row, (8, row.shape[1])))[:, :1]


def slopes(own, other, own_tags, other_tags, heat, bias):
    logit = heat * dot_nt(own, other) + bias
    return 1.0 / (1.0 + jnp.exp(-logit)) - jnp.where(own_tags == other_tags, 1.0, 0.0)


def pull(own, other, *tags_and_scalars):
    return dot_nn(halves(slopes(own, other, *tags_and_scalars)), other)


def scalars(heat_ref, bias_ref):
    return jnp.exp(jnp.full((1, 1), heat_ref[0], jnp.float32)), bias_ref[0]


def through_norm(total, unit, scale, heat):
    total = heat * total
    return scale * (total - unit * jnp.sum(unit * total, axis=-1, keepdims=True))


def put_tags(ref, tags):
    count = ref.shape[0] - 8
    ref[count:, :] = jnp.zeros((8, ref.shape[1]), jnp.float32)
    ref[count : count + 1, : tags.shape[1]] = tags


def is_even():
    return lax.rem(lax.axis_index("dp"), 2) == 0


def stage_kernel(caption_ref, tags_ref, out_ref):
    out_ref[: caption_ref.shape[0], :] = caption_ref[...]
    put_tags(out_ref, tags_ref[...].astype(jnp.float32).reshape(1, -1))


def unit_kernel(
    staged_ref, picture_ref,
    caption_out, picture_out, core_out, chip_out, own_tags_out, caption_scale, picture_scale, *parts,
):
    rows = picture_ref.shape[0]
    even = is_even()
    tags = staged_ref[rows : rows + 1, :rows]
    own_tags_out[...] = jnp.broadcast_to(column_of(tags), own_tags_out.shape)
    units = []
    for source, out, scale_out in (
        (staged_ref, caption_out, caption_scale),
        (picture_ref, picture_out, picture_scale),
    ):
        value = source[:rows, :]
        scale = inverse_norm(value)
        units.append(value * scale)
        out[...] = units[-1]
        scale_out[...] = jnp.broadcast_to(scale, scale_out.shape)
    caption, picture = units
    core_out[:rows, :] = jnp.where(even, caption, picture)
    put_tags(core_out, tags)
    chip = jnp.where(even, picture, caption)
    chip_out[:rows, :] = chip
    put_tags(chip_out, tags)
    step = rows // PARTS
    for k, part in enumerate(parts):
        part[:step, :] = chip[k * step : (k + 1) * step, :]
    put_tags(parts[0], tags)


def place_in_plane():
    return lax.rem(lax.axis_index("dp"), PLANE)


def own_kernel(
    heat_ref, bias_ref, own_tags_ref, staged_ref, caption_ref, picture_ref,
    caption_high_ref, caption_low_ref, picture_high_ref, picture_low_ref, c_ref, p_ref,
):
    heat, bias = scalars(heat_ref, bias_ref)
    rows = c_ref.shape[0]
    tags = staged_ref[rows : rows + 1, :rows]
    caption, picture = halves(caption_ref[...]), halves(picture_ref[...])
    caption_high_ref[...], caption_low_ref[...] = caption
    picture_high_ref[...], picture_low_ref[...] = picture
    slope = slopes(caption, picture, own_tags_ref[:, :1], tags, heat, bias)
    c_ref[...] = dot_nn(halves(slope), picture)
    p_ref[...] = dot_nn(halves(jnp.transpose(slope)), caption)


def far_kernel(heat_ref, bias_ref, own_tags_ref, high_ref, low_ref, far_ref, in_ref, out_ref):
    heat, bias = scalars(heat_ref, bias_ref)
    rows = out_ref.shape[0]
    other = far_ref[:rows, :]
    own, other = (high_ref[...], low_ref[...]), halves(other * inverse_norm(other))
    tags = far_ref[rows : rows + 1, :rows]
    out_ref[...] = in_ref[...] + pull(own, other, own_tags_ref[:, :1], tags, heat, bias)


def near_pull(heat, bias, own_tags_ref, caption, picture, of_caption, other_ref):
    rows = other_ref.shape[0] - 8
    own = [jnp.where(of_caption, c[...], p[...]) for c, p in zip(caption, picture, strict=True)]
    tags = other_ref[rows : rows + 1, :rows]
    return pull(own, halves(other_ref[:rows, :]), own_tags_ref[:, :1], tags, heat, bias)


def in_parts(place):
    return jnp.logical_or(place == 0, place == PLANE - 1)


def chip_kernel(
    heat_ref, bias_ref, own_tags_ref,
    caption_high_ref, caption_low_ref, picture_high_ref, picture_low_ref,
    other_ref, c_in_ref, p_in_ref, c_ref, p_ref,
):
    heat, bias = scalars(heat_ref, bias_ref)
    even = is_even()
    caption, picture = (caption_high_ref, caption_low_ref), (picture_high_ref, picture_low_ref)
    more = near_pull(heat, bias, own_tags_ref, caption, picture, jnp.logical_not(even), other_ref)
    more = jnp.where(in_parts(place_in_plane()), 0.0, more)
    c_ref[...] = c_in_ref[...] + jnp.where(even, 0.0, more)
    p_ref[...] = p_in_ref[...] + jnp.where(even, more, 0.0)


def core_kernel(
    heat_ref, bias_ref, own_tags_ref, picture_ref, scale_ref,
    caption_high_ref, caption_low_ref, picture_high_ref, picture_low_ref,
    other_ref, c_in_ref, p_in_ref, *refs,
):
    parts, (c_ref, p_ref, block) = refs[:PARTS], refs[PARTS:]
    heat, bias = scalars(heat_ref, bias_ref)
    rows = c_ref.shape[0]
    step = rows // PARTS
    even = is_even()
    caption, picture = (caption_high_ref, caption_low_ref), (picture_high_ref, picture_low_ref)
    more = near_pull(heat, bias, own_tags_ref, caption, picture, even, other_ref)
    c_ref[...] = c_in_ref[...] + jnp.where(even, more, 0.0)
    p_ref[...] = p_in_ref[...] + jnp.where(even, 0.0, more)

    @pl.when(in_parts(place_in_plane()))
    def _():
        for k, part in enumerate(parts):
            block[k * step : (k + 1) * step, :] = part[:step, :]
        block[rows:, :] = parts[0][step:, :]
        more = near_pull(heat, bias, own_tags_ref, caption, picture, jnp.logical_not(even), block)
        c_ref[...] += jnp.where(even, 0.0, more)
        p_ref[...] += jnp.where(even, more, 0.0)

    p_ref[...] = through_norm(p_ref[...], picture_ref[...], scale_ref[:, :1], heat)


def last_kernel(
    heat_ref, bias_ref, own_tags_ref, unit_ref, scale_ref, high_ref, low_ref, far_ref, tags_ref,
    in_ref, out_ref, block, sem,
):
    heat, bias = scalars(heat_ref, bias_ref)
    rows = block.shape[0]
    own, other = (high_ref[...], low_ref[...]), halves(far_ref[...])
    tags = tags_ref[rows : rows + 1, :rows]
    slope = halves(slopes(own, other, own_tags_ref[:, :1], tags, heat, bias))
    step = rows // BLOCKS
    copies = []
    for k in range(BLOCKS):
        at = pl.ds(k * step, step)
        part = [half[k * step : (k + 1) * step] for half in slope]
        total = in_ref[at, :] + dot_nn(part, other)
        block[at, :] = through_norm(total, unit_ref[at, :], scale_ref[at, :1], heat)
        copies.append(pltpu.make_async_copy(block.at[at, :], out_ref.at[at, :], sem.at[k]))
        copies[-1].start()
    for copy in copies:
        copy.wait()


def call(kernel, out_shape, *operands, cost=1024, scratch=(), hbm_out=False):
    return pl.pallas_call(
        kernel,
        out_shape=out_shape,
        in_specs=[SMEM if x.size == 1 else VMEM for x in operands],
        out_specs=[pl.BlockSpec(memory_space=pltpu.HBM) if hbm_out else VMEM] * len(out_shape),
        scratch_shapes=scratch,
        compiler_params=pltpu.CompilerParams(vmem_limit_bytes=24 * 1024 * 1024),
        cost_estimate=pl.CostEstimate(flops=cost, bytes_accessed=1024, transcendentals=0),
    )(*operands)


def local(picture, caption, tags, heat, bias):
    count = lax.axis_size("dp")
    rows, width = picture.shape
    step = rows // PARTS

    def f32(n, m=width):
        return jax.ShapeDtypeStruct((n, m), jnp.float32)

    def b16(n):
        return jax.ShapeDtypeStruct((n, width), jnp.bfloat16)

    def over_half(i):
        return i + count // 2

    (staged,) = call(stage_kernel, [f32(rows + 8)], caption, tags)
    far_caption = swap(staged, over_half)
    caption, picture, core, chip, own_tags, caption_scale, picture_scale, *parts = call(
        unit_kernel,
        [f32(rows)] * 2 + [f32(rows + 8)] * 2 + [f32(rows, 128)] * 3
        + [f32(step + 8)] + [f32(step)] * (PARTS - 1),
        staged, picture,
    )
    parts = [outward(part, k) for k, part in enumerate(parts)]
    parts = [homeward(part, k) for k, part in enumerate(parts)]
    core = swap(core, over_core)
    chip = swap(chip, over_chip)
    far_picture = swap(picture, over_half)
    scalar = heat, bias, own_tags
    *units, c, p = call(
        own_kernel, [b16(rows)] * 4 + [f32(rows)] * 2, *scalar, staged, caption, picture
    )
    (p,) = call(far_kernel, [f32(rows)], *scalar, *units[2:], far_caption, p, cost=FAR_COST)
    c, p = call(chip_kernel, [f32(rows)] * 2, *scalar, *units, chip, c, p)
    c, p = call(
        core_kernel, [f32(rows)] * 2,
        *scalar, picture, picture_scale, *units, core, c, p, *parts,
        scratch=[pltpu.VMEM((rows + 8, width), jnp.float32)],
    )
    (c,) = call(
        last_kernel, [f32(rows)],
        *scalar, caption, caption_scale, *units[:2], far_picture, far_caption, c,
        scratch=[pltpu.VMEM((rows, width), jnp.float32), pltpu.SemaphoreType.DMA((BLOCKS,))],
        hbm_out=True,
    )
    return p, c


def solution(mesh):
    return jax.shard_map(
        local,
        mesh=mesh,
        in_specs=(P("dp", None), P("dp", None), P("dp"), P(), P()),
        out_specs=(P("dp", None), P("dp", None)),
        check_vma=False,
    )
```

```python
import jax
import jax.numpy as jnp
from jax import lax
from jax.experimental import pallas as pl
from jax.experimental.pallas import tpu as pltpu
from jax.sharding import PartitionSpec as P

NT = (((1,), (1,)), ((), ()))
NN = (((1,), (0,)), ((), ()))
PLANE = 128
DEEP = 16
UP_BY = ((0, 15), (3, 0), (2, 15), (3, 14))
DOWN_BY = ((0, 15), (3, 0), (1, 0), (0, 1))
PARTS = len(UP_BY)
BLOCKS = 3
STAGES = 4
FAR_COST = 1 << 37
VMEM = pl.BlockSpec(memory_space=pltpu.VMEM)
SMEM = pl.BlockSpec(memory_space=pltpu.SMEM)


def swap(block, to):
    count = lax.axis_size("dp")
    route = [(i, to(i) % count) for i in range(count)]
    return lax.ppermute(block, "dp", [pair for pair in route if pair[0] != pair[1]])


def over_core(i):
    return i ^ 1


def over_chip(i):
    j = i + 1 if i % 2 else i - 1
    return j if i // PLANE == j // PLANE else i


def relays(k):
    up, down = UP_BY[k], DOWN_BY[k]
    return (up[0] * DEEP + up[1]) * 2, (down[0] * DEEP + down[1]) * 2 + 1


def outward(block, k):
    count = lax.axis_size("dp")
    up, down = relays(k)
    route = []
    for plane in range(0, count, PLANE):
        route.append((plane + PLANE - 1, (plane + PLANE) % count + up))
        route.append((plane, (plane - PLANE) % count + down))
    return lax.ppermute(block, "dp", route)


def homeward(block, k):
    count = lax.axis_size("dp")
    up, down = relays(k)
    route = []
    for plane in range(0, count, PLANE):
        route.append((plane + up, plane))
        route.append((plane + down, plane + PLANE - 1))
    return lax.ppermute(block, "dp", route)


def inverse_norm(rows):
    return lax.rsqrt(jnp.sum(rows * rows, axis=-1, keepdims=True) + 1e-06)


def halves(value):
    high = value.astype(jnp.bfloat16)
    low = (value - high.astype(jnp.float32)).astype(jnp.bfloat16)
    return high, low


def dot(left, right, dims):
    return lax.dot_general(left, right, dims, preferred_element_type=jnp.float32)


def dot_nt(left, right):
    count = right[0].shape[0]
    both = dot(left[0], jnp.concatenate(right, axis=0), NT)
    return both[:, :count] + (both[:, count:] + dot(left[1], right[0], NT))


def dot_nn(left, right):
    high, low = right
    left = jnp.concatenate([left[0], left[0], left[1]], axis=1)
    return dot(left, jnp.concatenate([high, low, high], axis=0), NN)


def column_of(row):
    return jnp.transpose(jnp.broadcast_to(row, (8, row.shape[1])))[:, :1]


def slopes(own, other, own_tags, other_tags, heat, bias):
    logit = heat * dot_nt(own, other) + bias
    return 1.0 / (1.0 + jnp.exp(-logit)) - jnp.where(own_tags == other_tags, 1.0, 0.0)


def pull(own, other, *tags_and_scalars):
    return dot_nn(halves(slopes(own, other, *tags_and_scalars)), other)


def scalars(heat_ref, bias_ref):
    return jnp.exp(jnp.full((1, 1), heat_ref[0], jnp.float32)), bias_ref[0]


def through_norm(total, unit, scale, heat):
    total = heat * total
    return scale * (total - unit * jnp.sum(unit * total, axis=-1, keepdims=True))


def put_tags(ref, tags):
    count = ref.shape[0] - 8
    ref[count:, :] = jnp.zeros((8, ref.shape[1]), jnp.float32)
    ref[count : count + 1, : tags.shape[1]] = tags


def is_even():
    return lax.rem(lax.axis_index("dp"), 2) == 0


def stage_kernel(caption_ref, tags_ref, out_ref, tags, sem):
    rows = caption_ref.shape[0]
    copies = [pltpu.make_async_copy(tags_ref, tags, sem.at[STAGES])]
    for k in range(STAGES):
        at = pl.ds(k * (rows // STAGES), rows // STAGES)
        copies.append(pltpu.make_async_copy(caption_ref.at[at, :], out_ref.at[at, :], sem.at[k]))
    for copy in copies:
        copy.start()
    copies[0].wait()
    put_tags(out_ref, tags[...].astype(jnp.float32).reshape(1, -1))
    for copy in copies[1:]:
        copy.wait()


def unit_kernel(
    staged_ref, picture_ref,
    caption_out, picture_out, core_out, chip_out, own_tags_out, caption_scale, picture_scale, *refs,
):
    parts, (raw, sem) = refs[:PARTS], refs[PARTS:]
    rows = picture_ref.shape[0]
    copy = pltpu.make_async_copy(picture_ref, raw, sem)
    copy.start()
    even = is_even()
    tags = staged_ref[rows : rows + 1, :rows]
    own_tags_out[...] = jnp.broadcast_to(column_of(tags), own_tags_out.shape)
    units = []
    for source, out, scale_out in (
        (staged_ref, caption_out, caption_scale),
        (raw, picture_out, picture_scale),
    ):
        if source is raw:
            copy.wait()
        value = source[:rows, :]
        scale = inverse_norm(value)
        units.append(value * scale)
        out[...] = units[-1]
        scale_out[...] = jnp.broadcast_to(scale, scale_out.shape)
    caption, picture = units
    core_out[:rows, :] = jnp.where(even, caption, picture)
    put_tags(core_out, tags)
    chip = jnp.where(even, picture, caption)
    chip_out[:rows, :] = chip
    put_tags(chip_out, tags)
    step = rows // PARTS
    for k, part in enumerate(parts):
        part[:step, :] = chip[k * step : (k + 1) * step, :]
    put_tags(parts[0], tags)


def place_in_plane():
    return lax.rem(lax.axis_index("dp"), PLANE)


def own_kernel(
    heat_ref, bias_ref, own_tags_ref, staged_ref, caption_ref, picture_ref,
    caption_high_ref, caption_low_ref, picture_high_ref, picture_low_ref, c_ref, p_ref,
):
    heat, bias = scalars(heat_ref, bias_ref)
    rows = c_ref.shape[0]
    tags = staged_ref[rows : rows + 1, :rows]
    caption, picture = halves(caption_ref[...]), halves(picture_ref[...])
    caption_high_ref[...], caption_low_ref[...] = caption
    picture_high_ref[...], picture_low_ref[...] = picture
    slope = slopes(caption, picture, own_tags_ref[:, :1], tags, heat, bias)
    c_ref[...] = dot_nn(halves(slope), picture)
    p_ref[...] = dot_nn(halves(jnp.transpose(slope)), caption)


def far_kernel(heat_ref, bias_ref, own_tags_ref, high_ref, low_ref, far_ref, in_ref, out_ref):
    heat, bias = scalars(heat_ref, bias_ref)
    rows = out_ref.shape[0]
    other = far_ref[:rows, :]
    own, other = (high_ref[...], low_ref[...]), halves(other * inverse_norm(other))
    tags = far_ref[rows : rows + 1, :rows]
    out_ref[...] = in_ref[...] + pull(own, other, own_tags_ref[:, :1], tags, heat, bias)


def near_pull(heat, bias, own_tags_ref, caption, picture, of_caption, other_ref):
    rows = other_ref.shape[0] - 8
    own = [jnp.where(of_caption, c[...], p[...]) for c, p in zip(caption, picture, strict=True)]
    tags = other_ref[rows : rows + 1, :rows]
    return pull(own, halves(other_ref[:rows, :]), own_tags_ref[:, :1], tags, heat, bias)


def in_parts(place):
    return jnp.logical_or(place == 0, place == PLANE - 1)


def chip_kernel(
    heat_ref, bias_ref, own_tags_ref,
    caption_high_ref, caption_low_ref, picture_high_ref, picture_low_ref,
    other_ref, c_in_ref, p_in_ref, c_ref, p_ref,
):
    heat, bias = scalars(heat_ref, bias_ref)
    even = is_even()
    caption, picture = (caption_high_ref, caption_low_ref), (picture_high_ref, picture_low_ref)
    more = near_pull(heat, bias, own_tags_ref, caption, picture, jnp.logical_not(even), other_ref)
    more = jnp.where(in_parts(place_in_plane()), 0.0, more)
    c_ref[...] = c_in_ref[...] + jnp.where(even, 0.0, more)
    p_ref[...] = p_in_ref[...] + jnp.where(even, more, 0.0)


def core_kernel(
    heat_ref, bias_ref, own_tags_ref, picture_ref, scale_ref,
    caption_high_ref, caption_low_ref, picture_high_ref, picture_low_ref,
    other_ref, c_in_ref, p_in_ref, *refs,
):
    parts, (c_ref, p_ref, block) = refs[:PARTS], refs[PARTS:]
    heat, bias = scalars(heat_ref, bias_ref)
    rows = c_ref.shape[0]
    step = rows // PARTS
    even = is_even()
    caption, picture = (caption_high_ref, caption_low_ref), (picture_high_ref, picture_low_ref)
    more = near_pull(heat, bias, own_tags_ref, caption, picture, even, other_ref)
    c_ref[...] = c_in_ref[...] + jnp.where(even, more, 0.0)
    p_ref[...] = p_in_ref[...] + jnp.where(even, 0.0, more)

    @pl.when(in_parts(place_in_plane()))
    def _():
        for k, part in enumerate(parts):
            block[k * step : (k + 1) * step, :] = part[:step, :]
        block[rows:, :] = parts[0][step:, :]
        more = near_pull(heat, bias, own_tags_ref, caption, picture, jnp.logical_not(even), block)
        c_ref[...] += jnp.where(even, 0.0, more)
        p_ref[...] += jnp.where(even, more, 0.0)

    p_ref[...] = through_norm(p_ref[...], picture_ref[...], scale_ref[:, :1], heat)


def last_kernel(
    heat_ref, bias_ref, own_tags_ref, unit_ref, scale_ref, high_ref, low_ref, far_ref, tags_ref,
    in_ref, out_ref, block, sem,
):
    heat, bias = scalars(heat_ref, bias_ref)
    rows = block.shape[0]
    own, other = (high_ref[...], low_ref[...]), halves(far_ref[...])
    tags = tags_ref[rows : rows + 1, :rows]
    slope = halves(slopes(own, other, own_tags_ref[:, :1], tags, heat, bias))
    step = rows // BLOCKS
    copies = []
    for k in range(BLOCKS):
        at = pl.ds(k * step, step)
        part = [half[k * step : (k + 1) * step] for half in slope]
        total = in_ref[at, :] + dot_nn(part, other)
        block[at, :] = through_norm(total, unit_ref[at, :], scale_ref[at, :1], heat)
        copies.append(pltpu.make_async_copy(block.at[at, :], out_ref.at[at, :], sem.at[k]))
        copies[-1].start()
    for copy in copies:
        copy.wait()


def call(kernel, out_shape, *operands, cost=1024, scratch=(), hbm_out=False):
    return pl.pallas_call(
        kernel,
        out_shape=out_shape,
        in_specs=[SMEM if x.size == 1 else VMEM for x in operands],
        out_specs=[pl.BlockSpec(memory_space=pltpu.HBM) if hbm_out else VMEM] * len(out_shape),
        scratch_shapes=scratch,
        compiler_params=pltpu.CompilerParams(vmem_limit_bytes=24 * 1024 * 1024),
        cost_estimate=pl.CostEstimate(flops=cost, bytes_accessed=1024, transcendentals=0),
    )(*operands)


def local(picture, caption, tags, heat, bias):
    count = lax.axis_size("dp")
    rows, width = picture.shape
    step = rows // PARTS

    def f32(n, m=width):
        return jax.ShapeDtypeStruct((n, m), jnp.float32)

    def b16(n):
        return jax.ShapeDtypeStruct((n, width), jnp.bfloat16)

    def over_half(i):
        return i + count // 2

    hbm = pl.BlockSpec(memory_space=pltpu.HBM)
    staged = pl.pallas_call(
        stage_kernel,
        out_shape=f32(rows + 8),
        in_specs=[hbm, hbm],
        out_specs=VMEM,
        scratch_shapes=[pltpu.VMEM(tags.shape, jnp.int32), pltpu.SemaphoreType.DMA((STAGES + 1,))],
        cost_estimate=pl.CostEstimate(flops=1024, bytes_accessed=1024, transcendentals=0),
        compiler_params=pltpu.CompilerParams(vmem_limit_bytes=24 * 1024 * 1024),
    )(*(pltpu.with_memory_space_constraint(x, pltpu.HBM) for x in (caption, tags)))
    far_caption = swap(staged, over_half)
    caption, picture, core, chip, own_tags, caption_scale, picture_scale, *parts = pl.pallas_call(
        unit_kernel,
        out_shape=[f32(rows)] * 2 + [f32(rows + 8)] * 2 + [f32(rows, 128)] * 3
        + [f32(step + 8)] + [f32(step)] * (PARTS - 1),
        in_specs=[VMEM, hbm],
        out_specs=[VMEM] * (7 + PARTS),
        scratch_shapes=[pltpu.VMEM((rows, width), jnp.float32), pltpu.SemaphoreType.DMA(())],
        cost_estimate=pl.CostEstimate(flops=1024, bytes_accessed=1024, transcendentals=0),
        compiler_params=pltpu.CompilerParams(vmem_limit_bytes=24 * 1024 * 1024),
    )(staged, pltpu.with_memory_space_constraint(picture, pltpu.HBM))
    parts = [outward(part, k) for k, part in enumerate(parts)]
    parts = [homeward(part, k) for k, part in enumerate(parts)]
    core = swap(core, over_core)
    chip = swap(chip, over_chip)
    far_picture = swap(picture, over_half)
    scalar = heat, bias, own_tags
    *units, c, p = call(
        own_kernel, [b16(rows)] * 4 + [f32(rows)] * 2, *scalar, staged, caption, picture
    )
    (p,) = call(far_kernel, [f32(rows)], *scalar, *units[2:], far_caption, p, cost=FAR_COST)
    c, p = call(chip_kernel, [f32(rows)] * 2, *scalar, *units, chip, c, p)
    c, p = call(
        core_kernel, [f32(rows)] * 2,
        *scalar, picture, picture_scale, *units, core, c, p, *parts,
        scratch=[pltpu.VMEM((rows + 8, width), jnp.float32)],
    )
    (c,) = call(
        last_kernel, [f32(rows)],
        *scalar, caption, caption_scale, *units[:2], far_picture, far_caption, c,
        scratch=[pltpu.VMEM((rows, width), jnp.float32), pltpu.SemaphoreType.DMA((BLOCKS,))],
        hbm_out=True,
    )
    return p, c


def solution(mesh):
    return jax.shard_map(
        local,
        mesh=mesh,
        in_specs=(P("dp", None), P("dp", None), P("dp"), P(), P()),
        out_specs=(P("dp", None), P("dp", None)),
        check_vma=False,
    )
```

```python
import jax
import jax.numpy as jnp
from jax import lax
from jax.experimental import pallas as pl
from jax.experimental.pallas import tpu as pltpu
from jax.sharding import PartitionSpec as P

NT = (((1,), (1,)), ((), ()))
NN = (((1,), (0,)), ((), ()))
PLANE = 128
DEEP = 16
UP_BY = ((0, 15), (3, 0), (2, 15), (3, 14))
DOWN_BY = ((0, 15), (3, 0), (1, 0), (0, 1))
PARTS = len(UP_BY)
BLOCKS = 3
STAGES = 4
FAR_COST = 1 << 37
VMEM = pl.BlockSpec(memory_space=pltpu.VMEM)
SMEM = pl.BlockSpec(memory_space=pltpu.SMEM)


def swap(block, to):
    count = lax.axis_size("dp")
    route = [(i, to(i) % count) for i in range(count)]
    return lax.ppermute(block, "dp", [pair for pair in route if pair[0] != pair[1]])


def over_core(i):
    return i ^ 1


def over_chip(i):
    j = i + 1 if i % 2 else i - 1
    return j if i // PLANE == j // PLANE else i


def relays(k):
    up, down = UP_BY[k], DOWN_BY[k]
    return (up[0] * DEEP + up[1]) * 2, (down[0] * DEEP + down[1]) * 2 + 1


def outward(block, k):
    count = lax.axis_size("dp")
    up, down = relays(k)
    route = []
    for plane in range(0, count, PLANE):
        route.append((plane + PLANE - 1, (plane + PLANE) % count + up))
        route.append((plane, (plane - PLANE) % count + down))
    return lax.ppermute(block, "dp", route)


def homeward(block, k):
    count = lax.axis_size("dp")
    up, down = relays(k)
    route = []
    for plane in range(0, count, PLANE):
        route.append((plane + up, plane))
        route.append((plane + down, plane + PLANE - 1))
    return lax.ppermute(block, "dp", route)


def inverse_norm(rows):
    return lax.rsqrt(jnp.sum(rows * rows, axis=-1, keepdims=True) + 1e-06)


def halves(value):
    high = value.astype(jnp.bfloat16)
    low = (value - high.astype(jnp.float32)).astype(jnp.bfloat16)
    return high, low


def dot(left, right, dims):
    return lax.dot_general(left, right, dims, preferred_element_type=jnp.float32)


def dot_nt(left, right):
    count = right[0].shape[0]
    both = dot(left[0], jnp.concatenate(right, axis=0), NT)
    return both[:, :count] + (both[:, count:] + dot(left[1], right[0], NT))


def dot_nn(left, right):
    high, low = right
    left = jnp.concatenate([left[0], left[0], left[1]], axis=1)
    return dot(left, jnp.concatenate([high, low, high], axis=0), NN)


def column_of(row):
    return jnp.transpose(jnp.broadcast_to(row, (8, row.shape[1])))[:, :1]


def slopes(own, other, own_tags, other_tags, heat, bias):
    logit = heat * dot_nt(own, other) + bias
    same = own_tags == other_tags
    slope = 1.0 / (1.0 + jnp.exp(jnp.where(same, logit, -logit)))
    return jnp.where(same, -slope, slope)


def pull(own, other, *tags_and_scalars):
    return dot_nn(halves(slopes(own, other, *tags_and_scalars)), other)


def scalars(heat_ref, bias_ref):
    return jnp.exp(jnp.full((1, 1), heat_ref[0], jnp.float32)), bias_ref[0]


def through_norm(total, unit, scale, heat):
    total = heat * total
    return scale * (total - unit * jnp.sum(unit * total, axis=-1, keepdims=True))


def put_tags(ref, tags):
    count = ref.shape[0] - 8
    ref[count:, :] = jnp.zeros((8, ref.shape[1]), jnp.float32)
    ref[count : count + 1, : tags.shape[1]] = tags


def is_even():
    return lax.rem(lax.axis_index("dp"), 2) == 0


def stage_kernel(caption_ref, tags_ref, out_ref, tags, sem):
    rows = caption_ref.shape[0]
    copies = [pltpu.make_async_copy(tags_ref, tags, sem.at[STAGES])]
    for k in range(STAGES):
        at = pl.ds(k * (rows // STAGES), rows // STAGES)
        copies.append(pltpu.make_async_copy(caption_ref.at[at, :], out_ref.at[at, :], sem.at[k]))
    for copy in copies:
        copy.start()
    copies[0].wait()
    put_tags(out_ref, tags[...].astype(jnp.float32).reshape(1, -1))
    for copy in copies[1:]:
        copy.wait()


def unit_kernel(
    staged_ref, picture_ref,
    caption_out, picture_out, core_out, chip_out, own_tags_out, caption_scale, picture_scale, *refs,
):
    parts, (raw, sem) = refs[:PARTS], refs[PARTS:]
    rows = picture_ref.shape[0]
    copy = pltpu.make_async_copy(picture_ref, raw, sem)
    copy.start()
    even = is_even()
    tags = staged_ref[rows : rows + 1, :rows]
    own_tags_out[...] = jnp.broadcast_to(column_of(tags), own_tags_out.shape)
    units = []
    for source, out, scale_out in (
        (staged_ref, caption_out, caption_scale),
        (raw, picture_out, picture_scale),
    ):
        if source is raw:
            copy.wait()
        value = source[:rows, :]
        scale = inverse_norm(value)
        units.append(value * scale)
        out[...] = units[-1]
        scale_out[...] = jnp.broadcast_to(scale, scale_out.shape)
    caption, picture = units
    core_out[:rows, :] = jnp.where(even, caption, picture)
    put_tags(core_out, tags)
    chip = jnp.where(even, picture, caption)
    chip_out[:rows, :] = chip
    put_tags(chip_out, tags)
    step = rows // PARTS
    for k, part in enumerate(parts):
        part[:step, :] = chip[k * step : (k + 1) * step, :]
    put_tags(parts[0], tags)


def place_in_plane():
    return lax.rem(lax.axis_index("dp"), PLANE)


def own_kernel(
    heat_ref, bias_ref, own_tags_ref, staged_ref, caption_ref, picture_ref,
    caption_high_ref, caption_low_ref, picture_high_ref, picture_low_ref, c_ref, p_ref,
):
    heat, bias = scalars(heat_ref, bias_ref)
    rows = c_ref.shape[0]
    tags = staged_ref[rows : rows + 1, :rows]
    caption, picture = halves(caption_ref[...]), halves(picture_ref[...])
    caption_high_ref[...], caption_low_ref[...] = caption
    picture_high_ref[...], picture_low_ref[...] = picture
    slope = slopes(caption, picture, own_tags_ref[:, :1], tags, heat, bias)
    c_ref[...] = dot_nn(halves(slope), picture)
    p_ref[...] = dot_nn(halves(jnp.transpose(slope)), caption)


def far_kernel(heat_ref, bias_ref, own_tags_ref, high_ref, low_ref, far_ref, in_ref, out_ref):
    heat, bias = scalars(heat_ref, bias_ref)
    rows = out_ref.shape[0]
    other = far_ref[:rows, :]
    own, other = (high_ref[...], low_ref[...]), halves(other * inverse_norm(other))
    tags = far_ref[rows : rows + 1, :rows]
    out_ref[...] = in_ref[...] + pull(own, other, own_tags_ref[:, :1], tags, heat, bias)


def near_pull(heat, bias, own_tags_ref, caption, picture, of_caption, other_ref):
    rows = other_ref.shape[0] - 8
    own = [jnp.where(of_caption, c[...], p[...]) for c, p in zip(caption, picture, strict=True)]
    tags = other_ref[rows : rows + 1, :rows]
    return pull(own, halves(other_ref[:rows, :]), own_tags_ref[:, :1], tags, heat, bias)


def in_parts(place):
    return jnp.logical_or(place == 0, place == PLANE - 1)


def chip_kernel(
    heat_ref, bias_ref, own_tags_ref,
    caption_high_ref, caption_low_ref, picture_high_ref, picture_low_ref,
    other_ref, c_in_ref, p_in_ref, c_ref, p_ref,
):
    heat, bias = scalars(heat_ref, bias_ref)
    even = is_even()
    caption, picture = (caption_high_ref, caption_low_ref), (picture_high_ref, picture_low_ref)
    more = near_pull(heat, bias, own_tags_ref, caption, picture, jnp.logical_not(even), other_ref)
    more = jnp.where(in_parts(place_in_plane()), 0.0, more)
    c_ref[...] = c_in_ref[...] + jnp.where(even, 0.0, more)
    p_ref[...] = p_in_ref[...] + jnp.where(even, more, 0.0)


def core_kernel(
    heat_ref, bias_ref, own_tags_ref, picture_ref, scale_ref,
    caption_high_ref, caption_low_ref, picture_high_ref, picture_low_ref,
    other_ref, c_in_ref, p_in_ref, *refs,
):
    parts, (c_ref, p_ref, block) = refs[:PARTS], refs[PARTS:]
    heat, bias = scalars(heat_ref, bias_ref)
    rows = c_ref.shape[0]
    step = rows // PARTS
    even = is_even()
    caption, picture = (caption_high_ref, caption_low_ref), (picture_high_ref, picture_low_ref)
    more = near_pull(heat, bias, own_tags_ref, caption, picture, even, other_ref)
    c_ref[...] = c_in_ref[...] + jnp.where(even, more, 0.0)
    p_ref[...] = p_in_ref[...] + jnp.where(even, 0.0, more)

    @pl.when(in_parts(place_in_plane()))
    def _():
        for k, part in enumerate(parts):
            block[k * step : (k + 1) * step, :] = part[:step, :]
        block[rows:, :] = parts[0][step:, :]
        more = near_pull(heat, bias, own_tags_ref, caption, picture, jnp.logical_not(even), block)
        c_ref[...] += jnp.where(even, 0.0, more)
        p_ref[...] += jnp.where(even, more, 0.0)

    p_ref[...] = through_norm(p_ref[...], picture_ref[...], scale_ref[:, :1], heat)


def last_kernel(
    heat_ref, bias_ref, own_tags_ref, unit_ref, scale_ref, high_ref, low_ref, far_ref, tags_ref,
    in_ref, out_ref, block, sem,
):
    heat, bias = scalars(heat_ref, bias_ref)
    rows = block.shape[0]
    own, other = (high_ref[...], low_ref[...]), halves(far_ref[...])
    tags = tags_ref[rows : rows + 1, :rows]
    slope = halves(slopes(own, other, own_tags_ref[:, :1], tags, heat, bias))
    step = rows // BLOCKS
    copies = []
    for k in range(BLOCKS):
        at = pl.ds(k * step, step)
        part = [half[k * step : (k + 1) * step] for half in slope]
        total = in_ref[at, :] + dot_nn(part, other)
        block[at, :] = through_norm(total, unit_ref[at, :], scale_ref[at, :1], heat)
        copies.append(pltpu.make_async_copy(block.at[at, :], out_ref.at[at, :], sem.at[k]))
        copies[-1].start()
    for copy in copies:
        copy.wait()


def call(kernel, out_shape, *operands, cost=1024, scratch=(), hbm_out=False):
    return pl.pallas_call(
        kernel,
        out_shape=out_shape,
        in_specs=[SMEM if x.size == 1 else VMEM for x in operands],
        out_specs=[pl.BlockSpec(memory_space=pltpu.HBM) if hbm_out else VMEM] * len(out_shape),
        scratch_shapes=scratch,
        compiler_params=pltpu.CompilerParams(vmem_limit_bytes=24 * 1024 * 1024),
        cost_estimate=pl.CostEstimate(flops=cost, bytes_accessed=1024, transcendentals=0),
    )(*operands)


def local(picture, caption, tags, heat, bias):
    count = lax.axis_size("dp")
    rows, width = picture.shape
    step = rows // PARTS

    def f32(n, m=width):
        return jax.ShapeDtypeStruct((n, m), jnp.float32)

    def b16(n):
        return jax.ShapeDtypeStruct((n, width), jnp.bfloat16)

    def over_half(i):
        return i + count // 2

    hbm = pl.BlockSpec(memory_space=pltpu.HBM)
    staged = pl.pallas_call(
        stage_kernel,
        out_shape=f32(rows + 8),
        in_specs=[hbm, hbm],
        out_specs=VMEM,
        scratch_shapes=[pltpu.VMEM(tags.shape, jnp.int32), pltpu.SemaphoreType.DMA((STAGES + 1,))],
        cost_estimate=pl.CostEstimate(flops=1024, bytes_accessed=1024, transcendentals=0),
        compiler_params=pltpu.CompilerParams(vmem_limit_bytes=24 * 1024 * 1024),
    )(*(pltpu.with_memory_space_constraint(x, pltpu.HBM) for x in (caption, tags)))
    far_caption = swap(staged, over_half)
    caption, picture, core, chip, own_tags, caption_scale, picture_scale, *parts = pl.pallas_call(
        unit_kernel,
        out_shape=[f32(rows)] * 2 + [f32(rows + 8)] * 2 + [f32(rows, 128)] * 3
        + [f32(step + 8)] + [f32(step)] * (PARTS - 1),
        in_specs=[VMEM, hbm],
        out_specs=[VMEM] * (7 + PARTS),
        scratch_shapes=[pltpu.VMEM((rows, width), jnp.float32), pltpu.SemaphoreType.DMA(())],
        cost_estimate=pl.CostEstimate(flops=1024, bytes_accessed=1024, transcendentals=0),
        compiler_params=pltpu.CompilerParams(vmem_limit_bytes=24 * 1024 * 1024),
    )(staged, pltpu.with_memory_space_constraint(picture, pltpu.HBM))
    parts = [outward(part, k) for k, part in enumerate(parts)]
    parts = [homeward(part, k) for k, part in enumerate(parts)]
    core = swap(core, over_core)
    chip = swap(chip, over_chip)
    far_picture = swap(picture, over_half)
    scalar = heat, bias, own_tags
    *units, c, p = call(
        own_kernel, [b16(rows)] * 4 + [f32(rows)] * 2, *scalar, staged, caption, picture
    )
    (p,) = call(far_kernel, [f32(rows)], *scalar, *units[2:], far_caption, p, cost=FAR_COST)
    c, p = call(chip_kernel, [f32(rows)] * 2, *scalar, *units, chip, c, p)
    c, p = call(
        core_kernel, [f32(rows)] * 2,
        *scalar, picture, picture_scale, *units, core, c, p, *parts,
        scratch=[pltpu.VMEM((rows + 8, width), jnp.float32)],
    )
    (c,) = call(
        last_kernel, [f32(rows)],
        *scalar, caption, caption_scale, *units[:2], far_picture, far_caption, c,
        scratch=[pltpu.VMEM((rows, width), jnp.float32), pltpu.SemaphoreType.DMA((BLOCKS,))],
        hbm_out=True,
    )
    return p, c


def solution(mesh):
    return jax.shard_map(
        local,
        mesh=mesh,
        in_specs=(P("dp", None), P("dp", None), P("dp"), P(), P()),
        out_specs=(P("dp", None), P("dp", None)),
        check_vma=False,
    )
```

```python
import jax
import jax.numpy as jnp
from jax import lax
from jax.experimental import pallas as pl
from jax.experimental.pallas import tpu as pltpu
from jax.sharding import PartitionSpec as P

NT = (((1,), (1,)), ((), ()))
NN = (((1,), (0,)), ((), ()))
PLANE = 128
DEEP = 16
UP_BY = ((0, 15), (3, 0), (2, 15))
DOWN_BY = ((0, 15), (3, 0), (1, 0))
ENDS = (0, 96, 192, 288, 384)
PARTS = len(ENDS) - 1
BLOCKS = 3
STAGES = 4
FAR_COST = 1 << 37
VMEM = pl.BlockSpec(memory_space=pltpu.VMEM)
SMEM = pl.BlockSpec(memory_space=pltpu.SMEM)


def swap(block, to):
    count = lax.axis_size("dp")
    route = [(i, to(i) % count) for i in range(count)]
    return lax.ppermute(block, "dp", [pair for pair in route if pair[0] != pair[1]])


def over_core(i):
    return i ^ 1


def over_chip(i):
    j = i + 1 if i % 2 else i - 1
    return j if i // PLANE == j // PLANE else i


def relays(k):
    up, down = UP_BY[k], DOWN_BY[k]
    return (up[0] * DEEP + up[1]) * 2, (down[0] * DEEP + down[1]) * 2 + 1


def outward(block, k):
    count = lax.axis_size("dp")
    up, down = relays(k) if k < len(UP_BY) else (0, PLANE - 1)
    route = []
    for plane in range(0, count, PLANE):
        route.append((plane + PLANE - 1, (plane + PLANE) % count + up))
        route.append((plane, (plane - PLANE) % count + down))
    return lax.ppermute(block, "dp", route)


def homeward(block, k):
    count = lax.axis_size("dp")
    up, down = relays(k)
    route = []
    for plane in range(0, count, PLANE):
        route.append((plane + up, plane))
        route.append((plane + down, plane + PLANE - 1))
    return lax.ppermute(block, "dp", route)


def inverse_norm(rows):
    return lax.rsqrt(jnp.sum(rows * rows, axis=-1, keepdims=True) + 1e-06)


def halves(value):
    high = value.astype(jnp.bfloat16)
    low = (value - high.astype(jnp.float32)).astype(jnp.bfloat16)
    return high, low


def dot(left, right, dims):
    return lax.dot_general(left, right, dims, preferred_element_type=jnp.float32)


def dot_nt(left, right):
    count = right[0].shape[0]
    both = dot(left[0], jnp.concatenate(right, axis=0), NT)
    return both[:, :count] + (both[:, count:] + dot(left[1], right[0], NT))


def dot_nn(left, right):
    high, low = right
    left = jnp.concatenate([left[0], left[0], left[1]], axis=1)
    return dot(left, jnp.concatenate([high, low, high], axis=0), NN)


def column_of(row):
    return jnp.transpose(jnp.broadcast_to(row, (8, row.shape[1])))[:, :1]


def slopes(own, other, own_tags, other_tags, heat, bias):
    logit = heat * dot_nt(own, other) + bias
    same = own_tags == other_tags
    slope = 1.0 / (1.0 + jnp.exp(jnp.where(same, logit, -logit)))
    return jnp.where(same, -slope, slope)


def pull(own, other, *tags_and_scalars):
    return dot_nn(halves(slopes(own, other, *tags_and_scalars)), other)


def scalars(heat_ref, bias_ref):
    return jnp.exp(jnp.full((1, 1), heat_ref[0], jnp.float32)), bias_ref[0]


def through_norm(total, unit, scale, heat):
    total = heat * total
    return scale * (total - unit * jnp.sum(unit * total, axis=-1, keepdims=True))


def put_tags(ref, tags):
    count = ref.shape[0] - 8
    ref[count:, :] = jnp.zeros((8, ref.shape[1]), jnp.float32)
    ref[count : count + 1, : tags.shape[1]] = tags


def is_even():
    return lax.rem(lax.axis_index("dp"), 2) == 0


def stage_kernel(caption_ref, tags_ref, out_ref, tags, sem):
    rows = caption_ref.shape[0]
    copies = [pltpu.make_async_copy(tags_ref, tags, sem.at[STAGES])]
    for k in range(STAGES):
        at = pl.ds(k * (rows // STAGES), rows // STAGES)
        copies.append(pltpu.make_async_copy(caption_ref.at[at, :], out_ref.at[at, :], sem.at[k]))
    for copy in copies:
        copy.start()
    copies[0].wait()
    put_tags(out_ref, tags[...].astype(jnp.float32).reshape(1, -1))
    for copy in copies[1:]:
        copy.wait()


def unit_kernel(
    staged_ref, picture_ref,
    caption_out, picture_out, core_out, chip_out, own_tags_out, caption_scale, picture_scale, *refs,
):
    parts, (raw, sem) = refs[:PARTS], refs[PARTS:]
    rows = picture_ref.shape[0]
    copy = pltpu.make_async_copy(picture_ref, raw, sem)
    copy.start()
    even = is_even()
    tags = staged_ref[rows : rows + 1, :rows]
    own_tags_out[...] = jnp.broadcast_to(column_of(tags), own_tags_out.shape)
    units = []
    for source, out, scale_out in (
        (staged_ref, caption_out, caption_scale),
        (raw, picture_out, picture_scale),
    ):
        if source is raw:
            copy.wait()
        value = source[:rows, :]
        scale = inverse_norm(value)
        units.append(value * scale)
        out[...] = units[-1]
        scale_out[...] = jnp.broadcast_to(scale, scale_out.shape)
    caption, picture = units
    core_out[:rows, :] = jnp.where(even, caption, picture)
    put_tags(core_out, tags)
    chip = jnp.where(even, picture, caption)
    chip_out[:rows, :] = chip
    put_tags(chip_out, tags)
    for k, part in enumerate(parts):
        part[: ENDS[k + 1] - ENDS[k], :] = chip[ENDS[k] : ENDS[k + 1], :]
    put_tags(parts[0], tags)


def place_in_plane():
    return lax.rem(lax.axis_index("dp"), PLANE)


def own_kernel(
    heat_ref, bias_ref, own_tags_ref, staged_ref, caption_ref, picture_ref,
    caption_high_ref, caption_low_ref, picture_high_ref, picture_low_ref, c_ref, p_ref,
):
    heat, bias = scalars(heat_ref, bias_ref)
    rows = c_ref.shape[0]
    tags = staged_ref[rows : rows + 1, :rows]
    caption, picture = halves(caption_ref[...]), halves(picture_ref[...])
    caption_high_ref[...], caption_low_ref[...] = caption
    picture_high_ref[...], picture_low_ref[...] = picture
    slope = slopes(caption, picture, own_tags_ref[:, :1], tags, heat, bias)
    c_ref[...] = dot_nn(halves(slope), picture)
    p_ref[...] = dot_nn(halves(jnp.transpose(slope)), caption)


def far_kernel(heat_ref, bias_ref, own_tags_ref, high_ref, low_ref, far_ref, in_ref, out_ref):
    heat, bias = scalars(heat_ref, bias_ref)
    rows = out_ref.shape[0]
    other = far_ref[:rows, :]
    own, other = (high_ref[...], low_ref[...]), halves(other * inverse_norm(other))
    tags = far_ref[rows : rows + 1, :rows]
    out_ref[...] = in_ref[...] + pull(own, other, own_tags_ref[:, :1], tags, heat, bias)


def near_pull(heat, bias, own_tags_ref, caption, picture, of_caption, other_ref):
    rows = other_ref.shape[0] - 8
    own = [jnp.where(of_caption, c[...], p[...]) for c, p in zip(caption, picture, strict=True)]
    tags = other_ref[rows : rows + 1, :rows]
    return pull(own, halves(other_ref[:rows, :]), own_tags_ref[:, :1], tags, heat, bias)


def in_parts(place):
    return jnp.logical_or(place == 0, place == PLANE - 1)


def chip_kernel(
    heat_ref, bias_ref, own_tags_ref,
    caption_high_ref, caption_low_ref, picture_high_ref, picture_low_ref,
    other_ref, c_in_ref, p_in_ref, c_ref, p_ref,
):
    heat, bias = scalars(heat_ref, bias_ref)
    even = is_even()
    caption, picture = (caption_high_ref, caption_low_ref), (picture_high_ref, picture_low_ref)
    more = near_pull(heat, bias, own_tags_ref, caption, picture, jnp.logical_not(even), other_ref)
    more = jnp.where(in_parts(place_in_plane()), 0.0, more)
    c_ref[...] = c_in_ref[...] + jnp.where(even, 0.0, more)
    p_ref[...] = p_in_ref[...] + jnp.where(even, more, 0.0)


def core_kernel(
    heat_ref, bias_ref, own_tags_ref, picture_ref, scale_ref,
    caption_high_ref, caption_low_ref, picture_high_ref, picture_low_ref,
    other_ref, c_in_ref, p_in_ref, *refs,
):
    parts, (c_ref, p_ref, block) = refs[:PARTS], refs[PARTS:]
    heat, bias = scalars(heat_ref, bias_ref)
    rows = c_ref.shape[0]
    even = is_even()
    caption, picture = (caption_high_ref, caption_low_ref), (picture_high_ref, picture_low_ref)
    more = near_pull(heat, bias, own_tags_ref, caption, picture, even, other_ref)
    c_ref[...] = c_in_ref[...] + jnp.where(even, more, 0.0)
    p_ref[...] = p_in_ref[...] + jnp.where(even, 0.0, more)

    @pl.when(in_parts(place_in_plane()))
    def _():
        for k, part in enumerate(parts):
            block[ENDS[k] : ENDS[k + 1], :] = part[: ENDS[k + 1] - ENDS[k], :]
        block[rows:, :] = parts[0][ENDS[1] :, :]
        more = near_pull(heat, bias, own_tags_ref, caption, picture, jnp.logical_not(even), block)
        c_ref[...] += jnp.where(even, 0.0, more)
        p_ref[...] += jnp.where(even, more, 0.0)

    p_ref[...] = through_norm(p_ref[...], picture_ref[...], scale_ref[:, :1], heat)


def last_kernel(
    heat_ref, bias_ref, own_tags_ref, unit_ref, scale_ref, high_ref, low_ref, far_ref, tags_ref,
    in_ref, out_ref, block, sem,
):
    heat, bias = scalars(heat_ref, bias_ref)
    rows = block.shape[0]
    own, other = (high_ref[...], low_ref[...]), halves(far_ref[...])
    tags = tags_ref[rows : rows + 1, :rows]
    slope = halves(slopes(own, other, own_tags_ref[:, :1], tags, heat, bias))
    step = rows // BLOCKS
    copies = []
    for k in range(BLOCKS):
        at = pl.ds(k * step, step)
        part = [half[k * step : (k + 1) * step] for half in slope]
        total = in_ref[at, :] + dot_nn(part, other)
        block[at, :] = through_norm(total, unit_ref[at, :], scale_ref[at, :1], heat)
        copies.append(pltpu.make_async_copy(block.at[at, :], out_ref.at[at, :], sem.at[k]))
        copies[-1].start()
    for copy in copies:
        copy.wait()


def call(kernel, out_shape, *operands, cost=1024, scratch=(), hbm_out=False):
    return pl.pallas_call(
        kernel,
        out_shape=out_shape,
        in_specs=[SMEM if x.size == 1 else VMEM for x in operands],
        out_specs=[pl.BlockSpec(memory_space=pltpu.HBM) if hbm_out else VMEM] * len(out_shape),
        scratch_shapes=scratch,
        compiler_params=pltpu.CompilerParams(vmem_limit_bytes=24 * 1024 * 1024),
        cost_estimate=pl.CostEstimate(flops=cost, bytes_accessed=1024, transcendentals=0),
    )(*operands)


def local(picture, caption, tags, heat, bias):
    count = lax.axis_size("dp")
    rows, width = picture.shape

    def f32(n, m=width):
        return jax.ShapeDtypeStruct((n, m), jnp.float32)

    def b16(n):
        return jax.ShapeDtypeStruct((n, width), jnp.bfloat16)

    def over_half(i):
        return i + count // 2

    hbm = pl.BlockSpec(memory_space=pltpu.HBM)
    staged = pl.pallas_call(
        stage_kernel,
        out_shape=f32(rows + 8),
        in_specs=[hbm, hbm],
        out_specs=VMEM,
        scratch_shapes=[pltpu.VMEM(tags.shape, jnp.int32), pltpu.SemaphoreType.DMA((STAGES + 1,))],
        cost_estimate=pl.CostEstimate(flops=1024, bytes_accessed=1024, transcendentals=0),
        compiler_params=pltpu.CompilerParams(vmem_limit_bytes=24 * 1024 * 1024),
    )(*(pltpu.with_memory_space_constraint(x, pltpu.HBM) for x in (caption, tags)))
    far_caption = swap(staged, over_half)
    caption, picture, core, chip, own_tags, caption_scale, picture_scale, *parts = pl.pallas_call(
        unit_kernel,
        out_shape=[f32(rows)] * 2 + [f32(rows + 8)] * 2 + [f32(rows, 128)] * 3
        + [f32(ENDS[1] + 8)] + [f32(ENDS[k + 1] - ENDS[k]) for k in range(1, PARTS)],
        in_specs=[VMEM, hbm],
        out_specs=[VMEM] * (7 + PARTS),
        scratch_shapes=[pltpu.VMEM((rows, width), jnp.float32), pltpu.SemaphoreType.DMA(())],
        cost_estimate=pl.CostEstimate(flops=1024, bytes_accessed=1024, transcendentals=0),
        compiler_params=pltpu.CompilerParams(vmem_limit_bytes=24 * 1024 * 1024),
    )(staged, pltpu.with_memory_space_constraint(picture, pltpu.HBM))
    parts = [outward(part, k) for k, part in enumerate(parts)]
    parts[:-1] = [homeward(part, k) for k, part in enumerate(parts[:-1])]
    core = swap(core, over_core)
    chip = swap(chip, over_chip)
    far_picture = swap(picture, over_half)
    scalar = heat, bias, own_tags
    *units, c, p = call(
        own_kernel, [b16(rows)] * 4 + [f32(rows)] * 2, *scalar, staged, caption, picture
    )
    (p,) = call(far_kernel, [f32(rows)], *scalar, *units[2:], far_caption, p, cost=FAR_COST)
    c, p = call(chip_kernel, [f32(rows)] * 2, *scalar, *units, chip, c, p)
    c, p = call(
        core_kernel, [f32(rows)] * 2,
        *scalar, picture, picture_scale, *units, core, c, p, *parts,
        scratch=[pltpu.VMEM((rows + 8, width), jnp.float32)],
    )
    (c,) = call(
        last_kernel, [f32(rows)],
        *scalar, caption, caption_scale, *units[:2], far_picture, far_caption, c,
        scratch=[pltpu.VMEM((rows, width), jnp.float32), pltpu.SemaphoreType.DMA((BLOCKS,))],
        hbm_out=True,
    )
    return p, c


def solution(mesh):
    return jax.shard_map(
        local,
        mesh=mesh,
        in_specs=(P("dp", None), P("dp", None), P("dp"), P(), P()),
        out_specs=(P("dp", None), P("dp", None)),
        check_vma=False,
    )
```
